512 devices in a mesh: band: 32 (over y, x, z_hi), tracer: 16 (over z_lo, core).
Axes of the slice: x: 4, y: 4, z: 16 (z_hi: 2, z_lo: 8; z = z_hi * 8 + z_lo), core: 2. Of those that a mesh axis runs over, the one named last changes fastest.
Arguments:
- tracer: float32 [16, 16, 256, 720], P(None, 'tracer', 'band'), may hold values from 0.1 to 10
- air_mass: bfloat16 [16, 16, 256, 720], P('tracer', None, 'band'), may hold values from 1 to 2
- fluxes: bfloat16 [16, 3, 16, 256, 720], P('tracer', None, None, 'band'), may hold values from -0.119628906 to 0.119628906
- diffusivity: bfloat16 [16, 16, 256, 720], P('tracer', None, 'band'), may hold values from 0.29882812 to 3
- input_slot: int32 [32], replicated, may hold values from 0 to 15, as said below
Outputs:
- new_tracer: float32 [16, 16, 256, 720], P(None, 'tracer', 'band')
The draws below stay inside these ranges and needn't reach their ends.
Inputs may be any that keep to these rules, and one draw needn't show every extreme that they name: `input_slot`: band b reads slot (b + s) mod 16, with one s for all bands.
All inputs are finite; a program needn't handle non-finite values.
Results may differ from the reference program's by a relative error of at most 0.0003.
Values may be sent and summed in bfloat16 or wider, within the bound.
A program may use at most 64 MiB of HBM per device.

```python
import math
import jax
import jax.numpy as jnp
from jax import lax

LON = 720
LEV = 16
LAT_DEV = 8
LAT = 256
NTRAC = 16
SLOTS = 16


def draw_input_slot(key, part):
    key = jax.random.fold_in(key, 7)
    offset = jax.random.randint(key, (), 0, SLOTS)
    return ((jnp.arange(LAT // LAT_DEV) + offset) % SLOTS).astype(jnp.int32)


def level_of(rng, dims, shards, smallest, top_value):
    def one(axis_at, parts):
        steps = jax.random.uniform(jax.random.fold_in(jax.random.fold_in(rng, 6), axis_at), (parts,), jnp.float32, smallest / len(shards), top_value / len(shards))
        return jnp.repeat(jnp.exp(steps), dims[axis_at] // parts).reshape((-1,) + (1,) * (len(dims) - axis_at - 1))

    level = one(*shards[0])
    for cut in shards[1:]:
        level = level * one(*cut)
    return level


def setup_inputs(seed: int = 0) -> dict:
    keys = jax.random.split(jax.random.key(seed), 6)
    tracer = jnp.clip(jnp.exp(math.log(10.0) - 4.6051702 * jax.random.uniform(keys[0], (LEV, NTRAC, LAT, LON), jnp.float32) ** level_of(keys[0], (LEV, NTRAC, LAT, LON), ((1, 16), (2, 32)), -0.2, 0.2)), 0.1, 10.0)
    air_mass = jnp.clip(jnp.exp(math.log(2.0) - 0.6931472 * jax.random.uniform(keys[1], (SLOTS, LEV, LAT, LON), jnp.float32) ** level_of(keys[1], (SLOTS, LEV, LAT, LON), ((0, 16), (2, 32)), -0.2, 0.2)), 1.0, 2.0).astype(jnp.bfloat16)
    fluxes = jnp.clip(jax.random.uniform(keys[2], (SLOTS, 3, LEV, LAT, LON), jnp.float32, -0.119628906, 0.119628906) * level_of(keys[2], (SLOTS, 3, LEV, LAT, LON), ((0, 16), (3, 32)), -0.4, 0.0), -0.119628906, 0.119628906).astype(jnp.bfloat16)
    diffusivity = jnp.clip(jnp.exp(math.log(3.0) - 2.306499 * jax.random.uniform(keys[3], (SLOTS, LEV, LAT, LON), jnp.float32) ** level_of(keys[3], (SLOTS, LEV, LAT, LON), ((0, 16), (2, 32)), -0.2, 0.2)), 0.29882812, 3.0).astype(jnp.bfloat16)
    input_slot = draw_input_slot(jax.random.fold_in(keys[5], 71), 0)
    return {"tracer": tracer, "air_mass": air_mass, "fluxes": fluxes, "diffusivity": diffusivity, "input_slot": input_slot}


def limited_slope(left, centre, right):
    down = centre - left
    rise = right - centre
    middle = 0.5 * (right - left)
    bound = jnp.minimum(jnp.minimum(jnp.abs(middle), 2.0 * jnp.abs(down)), 2.0 * jnp.abs(rise))
    return jnp.where(down * rise > 0.0, jnp.sign(down) * bound, 0.0)


def part_of(array, axis, lower, upper):
    return lax.slice_in_dim(array, lower, upper, axis=axis)


def advect(conc, mass, flux, axis):
    count = conc.shape[axis] - 4
    slope = limited_slope(part_of(conc, axis, 0, count + 2), part_of(conc, axis, 1, count + 3), part_of(conc, axis, 2, count + 4))
    face = part_of(flux, axis, 1, count + 2)
    left_c = part_of(conc, axis, 1, count + 2)
    right_c = part_of(conc, axis, 2, count + 3)
    left_m = part_of(mass, axis, 1, count + 2)
    right_m = part_of(mass, axis, 2, count + 3)
    left_s = part_of(slope, axis, 0, count + 1)
    right_s = part_of(slope, axis, 1, count + 2)
    forward = face * (left_c + 0.5 * (1.0 - face / left_m) * left_s)
    backward = face * (right_c - 0.5 * (1.0 + face / right_m) * right_s)
    moved = jnp.where(face > 0.0, forward, backward)
    inner_m = part_of(mass, axis, 2, count + 2)
    inner_c = part_of(conc, axis, 2, count + 2)
    new_mass = inner_m + part_of(face, axis, 0, count) - part_of(face, axis, 1, count + 1)
    new_amount = inner_m * inner_c + part_of(moved, axis, 0, count) - part_of(moved, axis, 1, count + 1)
    return new_amount / new_mass, new_mass


def wrap_x(array):
    return jnp.concatenate([array[..., -2:], array, array[..., :2]], axis=3)


def pad_axis(array, axis, value):
    widths = [(0, 0)] * array.ndim
    widths[axis] = (2, 2)
    return jnp.pad(array, widths, constant_values=value)


def diffuse(conc, mass, coupling):
    below = jnp.concatenate([jnp.zeros_like(coupling[:1]), coupling[:-1]], axis=0)
    diag = mass + below + coupling
    right_side = mass * conc

    def forward(carry, level):
        ratio_prev, value_prev = carry
        low, centre, upper_c, known = level
        pivot = centre - low * ratio_prev
        ratio = upper_c / pivot
        value = (known + low * value_prev) / pivot
        return (ratio, value), (ratio, value)

    start = (jnp.zeros(mass.shape[1:], jnp.float32), jnp.zeros(conc.shape[1:], jnp.float32))
    _, (ratios, values) = lax.scan(forward, start, (below, diag, coupling, right_side))

    def backward(above, level):
        ratio, value = level
        result = value + ratio * above
        return result, result

    _, solved = lax.scan(backward, jnp.zeros(conc.shape[1:], jnp.float32), (ratios, values), reverse=True)
    return solved


def reference(tracer, air_mass, fluxes, diffusivity, input_slot):
    levels = tracer.shape[0]
    rows = tracer.shape[2]
    width = tracer.shape[3]
    slot_row = input_slot[jnp.arange(rows) // LAT_DEV].astype(jnp.int32)
    pick = jnp.broadcast_to(slot_row.reshape(1, 1, rows, 1), (1, levels, rows, width))
    pick_flux = jnp.broadcast_to(slot_row.reshape(1, 1, 1, rows, 1), (1, 3, levels, rows, width))
    mass0 = jnp.take_along_axis(air_mass, pick, axis=0)[0].astype(jnp.float32)[:, None]
    coupling = jnp.take_along_axis(diffusivity, pick, axis=0)[0].astype(jnp.float32)[:, None]
    flux_rows = jnp.take_along_axis(fluxes, pick_flux, axis=0)[0].astype(jnp.float32)
    east = flux_rows[0][:, None]
    row_keep = (jnp.arange(rows) < rows - 1)[None, None, :, None]
    level_keep = (jnp.arange(levels) < levels - 1)[:, None, None, None]
    north = jnp.where(row_keep, flux_rows[1][:, None], 0.0)
    upper = jnp.where(level_keep, flux_rows[2][:, None], 0.0)
    coupling = jnp.where(level_keep, coupling, 0.0)
    conc1, mass1 = advect(wrap_x(tracer), wrap_x(mass0), wrap_x(east), 3)
    conc2, mass2 = advect(pad_axis(conc1, 2, 0.0), pad_axis(mass1, 2, 1.0), pad_axis(north, 2, 0.0), 2)
    conc3, mass3 = advect(pad_axis(conc2, 0, 0.0), pad_axis(mass2, 0, 1.0), pad_axis(upper, 0, 0.0), 0)
    return diffuse(conc3, mass3, coupling)
```

```python
import functools

import jax
import jax.numpy as jnp
from jax import lax
from jax.experimental import pallas as pl
from jax.experimental.pallas import tpu as pltpu
from jax.sharding import PartitionSpec as P

MESH = pl.DeviceIdType.MESH
LEV = 16
ROWS = 8
LON = 720
WIDE = 768
LANE = 128
BANDS = 32
SLOTS = 16
CHIPS = 8
CELLS = LEV * ROWS
CHUNK = 4
PER_FIELD = LEV // CHUNK
NCHUNK = 5 * PER_FIELD
BELOW = 5
ABOVE = 4


def row_plane(stage, row):
    parts = [stage[j, pl.ds(row, LEV, stride=ROWS), :] for j in range(WIDE // LANE)]
    parts[-1] = parts[-1][:, :LON % LANE]
    return jnp.concatenate(parts, axis=1).astype(jnp.bfloat16)


def fill_stage(stage, field):
    for j in range(WIDE // LANE):
        width = min(LANE, LON - j * LANE)
        stage[j, :, :width] = field[:, j * LANE:j * LANE + width]


def comm_kernel(
    shift, x_ref, mass_ref, flux_ref, coup_ref, met, edge, halo,
    hsend, esend, stage, local_sem, main_recv, main_send, halo_sem, edge_recv, edge_send,
):
    b = lax.axis_index("band")
    t = lax.axis_index("tracer")
    z = t // 2
    c = t % 2
    root = (b + shift) % SLOTS
    k = root // 2
    root_core = root % 2
    is_root = t == root
    at_root = z == k
    mate = t + 1 - 2 * c
    has_below = b > 0
    has_above = b < BANDS - 1
    side = jnp.where(z >= k, 1, -1)
    pos = jnp.where(z >= k, z - k, k - z)
    length = jnp.where(z >= k, CHIPS - 1 - k, k)
    hub = jnp.logical_and(pos > 0, pos % 2 == 0)
    child_far = jnp.logical_and(hub, pos + 2 <= length)
    child_back = hub
    child_last = jnp.logical_and(hub, pos + 1 == length)
    odd_parent = jnp.where(pos < length, pos + 1, pos - 1)
    parent_pos = jnp.where(pos % 2 == 0, pos - 2, odd_parent)
    parent_z = k + side * parent_pos
    up_step = jnp.minimum(CHIPS - 1 - k, 2)
    down_step = jnp.minimum(k, 2)
    root_up = jnp.logical_and(is_root, up_step > 0)
    root_down = jnp.logical_and(is_root, down_step > 0)
    one = lambda flag: jnp.where(flag, 1, 0)

    edge_hub = jnp.logical_or(z == 2, z == 5)
    hub_z = jnp.where(z < 4, 2, 5)
    far_z = jnp.where(z == 2, 0, 7)

    barrier = pltpu.get_barrier_semaphore()

    def greet(band, tracer, flag=None):
        def go():
            pl.semaphore_signal(barrier, inc=1, device_id={"band": band, "tracer": tracer}, device_id_type=MESH)

        if flag is None:
            go()
        else:
            pl.when(flag)(go)

    greet(b, mate)
    main_parent = jnp.where(parent_z == k, root, parent_z * 2 + c)
    greet(b, main_parent, jnp.logical_not(at_root))
    greet(b - 1, t, has_below)
    greet(b + 1, t, has_above)
    greet(b, hub_z * 2 + c, jnp.logical_not(edge_hub))
    greet(b - 1, (root + SLOTS - 1) % SLOTS, edge_hub & (c == 0) & has_below)
    greet(b + 1, (root + 1) % SLOTS, edge_hub & (c == 1) & has_above)
    expect = (
        1
        + one(has_below) + one(has_above)
        + one(child_far) + one(child_back) + one(child_last)
        + 2 * one(root_up) + 2 * one(root_down)
        + 3 * one(edge_hub)
        + 2 * one(is_root & has_below) + 2 * one(is_root & has_above)
    )

    loads = (
        pltpu.make_async_copy(mass_ref.at[0], met.at[0], local_sem.at[0]),
        pltpu.make_async_copy(flux_ref.at[0], met.at[pl.ds(1, 3)], local_sem.at[1]),
        pltpu.make_async_copy(coup_ref.at[0], met.at[4], local_sem.at[2]),
    )

    @pl.when(is_root)
    def _():
        for load in loads:
            load.start()

    pl.semaphore_wait(barrier, expect)

    def piece(i):
        return met.at[i // PER_FIELD, pl.ds(i % PER_FIELD * CHUNK, CHUNK)]

    def main_copy(i, which, tracer):
        return pltpu.make_async_remote_copy(
            src_ref=piece(i), dst_ref=piece(i),
            send_sem=main_send.at[which, i], recv_sem=main_recv.at[i],
            device_id={"band": b, "tracer": tracer}, device_id_type=MESH,
        )

    def start_if(flag, copy):
        pl.when(flag)(copy.start)

    @pl.when(is_root)
    def _():
        for load in loads:
            load.wait()

        def send(i, _):
            core = i % 2
            start_if(root_up, main_copy(i, 0, (z + up_step) * 2 + core))
            start_if(root_down, main_copy(i, 1, (z - down_step) * 2 + core))
            main_copy(i, 3, mate).start()
            return 0

        lax.fori_loop(0, NCHUNK, send, 0)

    fill_stage(stage, x_ref[...].reshape(CELLS, LON))
    for plane, row in enumerate((ROWS - 2, ROWS - 1, 0, 1)):
        hsend[plane] = row_plane(stage, row)

    def halo_copy(lower, band):
        part = pl.ds(0 if lower else 2, 2)
        return pltpu.make_async_remote_copy(
            src_ref=hsend.at[part], dst_ref=halo.at[part],
            send_sem=halo_sem.at[0 if lower else 1], recv_sem=halo_sem.at[2 if lower else 3],
            device_id={"band": band, "tracer": t}, device_id_type=MESH,
        )

    to_above = halo_copy(True, b + 1)
    to_below = halo_copy(False, b - 1)
    start_if(has_above, to_above)
    start_if(has_below, to_below)

    below_part = pl.ds(0, BELOW)
    above_part = pl.ds(BELOW, ABOVE)

    def edge_copy(which, lower, band, tracer, own):
        part = below_part if lower else above_part
        source = (esend if own else edge).at[part]
        return pltpu.make_async_remote_copy(
            src_ref=source, dst_ref=edge.at[part],
            send_sem=edge_send.at[which], recv_sem=edge_recv.at[0 if lower else 1],
            device_id={"band": band, "tracer": tracer}, device_id_type=MESH,
        )

    edge_out = (
        (is_root & has_above, edge_copy(0, True, b + 1, 4, True)),
        (is_root & has_above, edge_copy(1, True, b + 1, 10, True)),
        (is_root & has_below, edge_copy(2, False, b - 1, 5, True)),
        (is_root & has_below, edge_copy(3, False, b - 1, 11, True)),
    )

    @pl.when(is_root)
    def _():
        plan = (
            (0, ((ROWS - 2, 0), (ROWS - 1, 1), (0, 5), (1, 6))),
            (1, ((ROWS - 2, 2), (ROWS - 1, 3), (0, 7), (1, 8))),
            (2, ((ROWS - 1, 4),)),
        )
        for field, places in plan:
            fill_stage(stage, met[field].astype(jnp.float32).reshape(CELLS, LON))
            for row, place in places:
                esend[place] = row_plane(stage, row)
        for flag, copy in edge_out:
            start_if(flag, copy)

    relay = jnp.logical_not(at_root)

    def handed(i):
        return (
            (child_far, main_copy(i, 0, (z + 2 * side) * 2 + c)),
            (child_back, main_copy(i, 1, (z - side) * 2 + c)),
            (child_last, main_copy(i, 2, (z + side) * 2 + c)),
            (relay, main_copy(i, 3, mate)),
        )

    @pl.when(relay)
    def _():
        def step(j, _):
            i = 2 * j + c
            main_copy(i, 0, mate).wait_recv()
            for flag, copy in handed(i):
                start_if(flag, copy)
            return 0

        lax.fori_loop(0, NCHUNK // 2, step, 0)

    def edge_relay(lower):
        return (
            (edge_hub, edge_copy(4, lower, b, (z - 1) * 2 + c, False)),
            (edge_hub, edge_copy(5, lower, b, (z + 1) * 2 + c, False)),
            (edge_hub, edge_copy(6, lower, b, far_z * 2 + c, False)),
            (None, edge_copy(7, lower, b, mate, False)),
        )

    for lower, present in ((True, has_below), (False, has_above)):
        @pl.when(present & (c == (0 if lower else 1)))
        def _(lower=lower):
            edge_copy(0, lower, b, mate, False).wait_recv()
            for flag, copy in edge_relay(lower):
                if flag is None:
                    copy.start()
                else:
                    start_if(flag, copy)

    for lower, present in ((True, has_below), (False, has_above)):
        @pl.when(present & (c == (1 if lower else 0)))
        def _(lower=lower):
            edge_copy(0, lower, b, mate, False).wait_recv()

        @pl.when(present & (c == (0 if lower else 1)))
        def _(lower=lower):
            for flag, copy in edge_relay(lower):
                if flag is None:
                    copy.wait_send()
                else:
                    pl.when(flag)(copy.wait_send)

    pl.when(has_below)(to_above.wait_recv)
    pl.when(has_above)(to_below.wait_recv)
    pl.when(has_above)(to_above.wait_send)
    pl.when(has_below)(to_below.wait_send)
    for flag, copy in edge_out:
        pl.when(flag)(copy.wait_send)

    @pl.when(is_root)
    def _():
        def done(i, _):
            pl.when(root_up)(main_copy(i, 0, mate).wait_send)
            pl.when(root_down)(main_copy(i, 1, mate).wait_send)
            main_copy(i, 3, mate).wait_send()
            return 0

        lax.fori_loop(0, NCHUNK, done, 0)

    @pl.when(relay)
    def _():
        def done(j, _):
            main_copy(2 * j + 1 - c, 0, mate).wait_recv()
            for flag, copy in handed(2 * j + c):
                pl.when(flag)(copy.wait_send)
            return 0

        lax.fori_loop(0, NCHUNK // 2, done, 0)

    @pl.when(at_root & jnp.logical_not(is_root))
    def _():
        def done(i, _):
            main_copy(i, 0, mate).wait_recv()
            return 0

        lax.fori_loop(0, NCHUNK, done, 0)


def comm(shift, tracer, mass, flux, coup):
    vmem = pl.BlockSpec(memory_space=pltpu.VMEM)
    hbm = pl.BlockSpec(memory_space=pl.ANY)
    return pl.pallas_call(
        functools.partial(comm_kernel, shift),
        out_shape=(
            jax.ShapeDtypeStruct((5, LEV, ROWS, LON), jnp.bfloat16),
            jax.ShapeDtypeStruct((BELOW + ABOVE, LEV, LON), jnp.bfloat16),
            jax.ShapeDtypeStruct((4, LEV, LON), jnp.bfloat16),
        ),
        in_specs=[vmem, hbm, hbm, hbm],
        out_specs=(vmem, vmem, vmem),
        scratch_shapes=[
            pltpu.VMEM((4, LEV, LON), jnp.bfloat16),
            pltpu.VMEM((BELOW + ABOVE, LEV, LON), jnp.bfloat16),
            pltpu.VMEM((WIDE // LANE, CELLS, LANE), jnp.float32),
            pltpu.SemaphoreType.DMA((3,)),
            pltpu.SemaphoreType.DMA((NCHUNK,)),
            pltpu.SemaphoreType.DMA((4, NCHUNK)),
            pltpu.SemaphoreType.DMA((4,)),
            pltpu.SemaphoreType.DMA((2,)),
            pltpu.SemaphoreType.DMA((8,)),
        ],
        compiler_params=pltpu.CompilerParams(
            collective_id=shift, has_side_effects=True, vmem_limit_bytes=24 << 20
        ),
        name="exchange",
    )(tracer, mass, flux, coup)


def extended(x):
    spare = (WIDE - LON) // 2
    return jnp.concatenate([x, x[:, :spare], x[:, LON - spare:]], axis=1)


def doubled_slope(down, rise):
    middle = down + rise
    down, rise = 4.0 * down, 4.0 * rise
    positive = jnp.maximum(jnp.minimum(jnp.minimum(middle, down), rise), 0.0)
    negative = jnp.minimum(jnp.maximum(jnp.maximum(middle, down), rise), 0.0)
    return positive + negative


def advect_x(conc, mass, east):
    left = lambda v: pltpu.roll(v, 1, 1)
    right = lambda v: pltpu.roll(v, WIDE - 1, 1)
    rise = right(conc) - conc
    slope = doubled_slope(left(rise), rise)
    inverse = 1.0 / mass
    west = left(east)
    ahead = conc + 0.25 * (1.0 - east * inverse) * slope
    behind = conc - 0.25 * (1.0 + west * inverse) * slope
    moved = east * jnp.where(east > 0.0, ahead, right(behind))
    new_mass = mass + west - east
    new_amount = mass * conc + left(moved) - moved
    return new_amount / new_mass, new_mass


def compute_kernel(x_ref, met, edge, halo, out, conc2, mass2, ratio, value, side_c, side_m, side_f):
    b = lax.axis_index("band")
    f32 = jnp.float32
    lowest, highest = b == 0, b == BANDS - 1

    def plane(i):
        return extended(edge[i].astype(f32))

    for at, mass_at, east_at, out_of in ((0, 0, 2, lowest), (1, 1, 3, lowest), (2, 5, 7, highest), (3, 6, 8, highest)):
        conc, mass = advect_x(extended(halo[at].astype(f32)), plane(mass_at), plane(east_at))
        side_c[at] = jnp.where(out_of, 0.0, conc)
        if at in (1, 2):
            side_m[at - 1] = jnp.where(out_of, 1.0, mass)
    side_f[...] = jnp.where(lowest, 0.0, plane(4))

    row = lax.broadcasted_iota(jnp.int32, (ROWS, WIDE), 0)
    first, last = row == 0, row == ROWS - 1
    sign = jnp.where(first, 1.0, -1.0)
    closed = jnp.logical_and(last, highest)

    def horizontal(lev, _):
        def field(i):
            return extended(met[i, lev].astype(f32))

        def spread(ref, *at):
            return jnp.broadcast_to(ref[(*at, pl.ds(lev, 1), slice(None))].reshape(1, WIDE), (ROWS, WIDE))

        conc, mass = advect_x(extended(x_ref[lev]), field(0), field(1))
        north = jnp.where(closed, 0.0, field(2))
        c_before, c_after = spread(side_c, 1), spread(side_c, 2)
        f_before = spread(side_f)
        lower = lambda v: pltpu.roll(v, 1, 0)
        higher = lambda v: pltpu.roll(v, ROWS - 1, 0)
        down = conc - jnp.where(first, c_before, lower(conc))
        rise = jnp.where(last, c_after, higher(conc)) - conc
        slope = doubled_slope(down, rise)
        inverse = 1.0 / mass
        south = jnp.where(first, f_before, lower(north))
        ahead = conc + 0.25 * (1.0 - north * inverse) * slope
        behind = conc - 0.25 * (1.0 + south * inverse) * slope
        c_out = jnp.where(first, c_before, c_after)
        low_out = jnp.where(last, conc, spread(side_c, 0))
        high_out = jnp.where(first, conc, spread(side_c, 3))
        f_out = jnp.where(first, f_before, north)
        m_out = jnp.where(first, spread(side_m, 0), spread(side_m, 1))
        s_out = doubled_slope(c_out - low_out, high_out - c_out)
        from_out = c_out + 0.25 * (sign - f_out / m_out) * s_out
        moved = north * jnp.where(north > 0.0, ahead, jnp.where(last, from_out, higher(behind)))
        entering = f_before * jnp.where(f_before > 0.0, from_out, behind)
        new_mass = mass + south - north
        new_amount = mass * conc + jnp.where(first, entering, lower(moved)) - moved
        conc2[lev] = new_amount / new_mass
        mass2[lev] = new_mass
        return 0

    lax.fori_loop(0, LEV, horizontal, 0)
    zero = jnp.zeros((ROWS, WIDE), f32)
    for beyond in range(2):
        conc2[LEV + beyond] = zero
    mass2[LEV] = zero + 1.0

    def vertical(lev, carry):
        slope, c_below, flux_below, moved_below, k_below, ratio_prev, value_prev = carry
        inside = lev < LEV - 1
        flux = jnp.where(inside, extended(met[3, lev].astype(f32)), 0.0)
        k_above = jnp.where(inside, extended(met[4, lev].astype(f32)), 0.0)
        conc, above = conc2[lev], conc2[lev + 1]
        mass, mass_above = mass2[lev], mass2[lev + 1]
        slope_above = doubled_slope(above - conc, conc2[lev + 2] - above)
        up = flux > 0.0
        upwind_m = jnp.where(up, mass, mass_above)
        upwind_c = jnp.where(up, conc, above)
        upwind_s = jnp.where(up, slope, -slope_above)
        moved = flux * (upwind_c + 0.25 * (1.0 - jnp.abs(flux) / upwind_m) * upwind_s)
        new_mass = mass + flux_below - flux
        amount = mass * conc + moved_below - moved
        pivot = 1.0 / (new_mass + k_below + k_above - k_below * ratio_prev)
        ratio_here = k_above * pivot
        value_here = (amount + k_below * value_prev) * pivot
        ratio[lev] = ratio_here
        value[lev] = value_here
        return slope_above, conc, flux, moved, k_above, ratio_here, value_here

    first_slope = doubled_slope(conc2[0], conc2[1] - conc2[0])
    lax.fori_loop(0, LEV, vertical, (first_slope, zero, zero, zero, zero, zero, zero))

    def back(i, above):
        lev = LEV - 1 - i
        result = value[lev] + ratio[lev] * above
        out[lev] = result[:, :LON]
        return result

    lax.fori_loop(0, LEV, back, zero)


def compute(tracer, met, edge, halo):
    vmem = pl.BlockSpec(memory_space=pltpu.VMEM)
    f32 = jnp.float32
    return pl.pallas_call(
        compute_kernel,
        out_shape=jax.ShapeDtypeStruct((LEV, ROWS, LON), f32),
        in_specs=[vmem] * 4,
        out_specs=vmem,
        scratch_shapes=[
            pltpu.VMEM((LEV + 2, ROWS, WIDE), f32),
            pltpu.VMEM((LEV + 1, ROWS, WIDE), f32),
            pltpu.VMEM((LEV, ROWS, WIDE), f32),
            pltpu.VMEM((LEV, ROWS, WIDE), f32),
            pltpu.VMEM((4, LEV, WIDE), f32),
            pltpu.VMEM((2, LEV, WIDE), f32),
            pltpu.VMEM((LEV, WIDE), f32),
        ],
        compiler_params=pltpu.CompilerParams(vmem_limit_bytes=24 << 20),
        name="transport",
    )(tracer, met, edge, halo)


def per_device(tracer, air_mass, fluxes, diffusivity, input_slot):
    held = tracer.reshape(LEV, ROWS, LON)
    branches = [functools.partial(comm, shift) for shift in range(SLOTS)]
    met, edge, halo = lax.switch(input_slot[0], branches, held, air_mass, fluxes, diffusivity)
    return compute(held, met, edge, halo).reshape(tracer.shape)


def solution(mesh):
    placed = (
        P(None, "tracer", "band", None),
        P("tracer", None, "band", None),
        P("tracer", None, None, "band", None),
        P("tracer", None, "band", None),
        P(),
    )
    return jax.shard_map(
        per_device,
        mesh=mesh,
        in_specs=placed,
        out_specs=P(None, "tracer", "band", None),
        check_vma=False,
    )
```

```python
import functools

import jax
import jax.numpy as jnp
from jax import lax
from jax.experimental import pallas as pl
from jax.experimental.pallas import tpu as pltpu
from jax.sharding import PartitionSpec as P

MESH = pl.DeviceIdType.MESH
LEV = 16
ROWS = 8
LON = 720
WIDE = 768
LANE = 128
BANDS = 32
SLOTS = 16
CHIPS = 8
CELLS = LEV * ROWS
CHUNK = 4
PER_FIELD = LEV // CHUNK
NCHUNK = 5 * PER_FIELD
BELOW = 5
ABOVE = 4


def extended(x):
    spare = (WIDE - LON) // 2
    return jnp.concatenate([x, x[:, :spare], x[:, LON - spare:]], axis=1)


def padded(x):
    return jnp.concatenate([x, jnp.zeros((x.shape[0], WIDE - LON), x.dtype)], axis=1)


def inverse_of(x):
    return pl.reciprocal(x, approx=True)


def doubled_slope(down, rise):
    middle = down + rise
    down, rise = 4.0 * down, 4.0 * rise
    positive = jnp.maximum(jnp.minimum(jnp.minimum(middle, down), rise), 0.0)
    negative = jnp.minimum(jnp.maximum(jnp.maximum(middle, down), rise), 0.0)
    return positive + negative


def advect_x(conc, mass, east):
    left = lambda v: pltpu.roll(v, 1, 1)
    right = lambda v: pltpu.roll(v, WIDE - 1, 1)
    rise = right(conc) - conc
    slope = 0.25 * doubled_slope(left(rise), rise)
    inverse = inverse_of(mass)
    west = left(east)
    ahead = conc + (1.0 - east * inverse) * slope
    behind = conc - (1.0 + west * inverse) * slope
    moved = east * jnp.where(east > 0.0, ahead, right(behind))
    new_mass = mass + west - east
    new_amount = mass * conc + left(moved) - moved
    inverse = inverse_of(new_mass)
    return new_amount * inverse, new_mass, inverse


def side_planes(edge, halo, side_c, side_i, side_f, lowest, highest):
    f32 = jnp.float32

    def plane(i):
        return extended(edge[i].astype(f32))

    for at, mass_at, east_at, out_of in ((0, 0, 2, lowest), (1, 1, 3, lowest), (2, 5, 7, highest), (3, 6, 8, highest)):
        conc, _, inverse = advect_x(extended(halo[at].astype(f32)), plane(mass_at), plane(east_at))
        side_c[at] = jnp.where(out_of, 0.0, conc)
        if at in (1, 2):
            side_i[at - 1] = jnp.where(out_of, 1.0, inverse)
    side_f[...] = jnp.where(lowest, 0.0, plane(4))


def longitude(lev, x_ref, met, conc1, mass1, inverse1):
    f32 = jnp.float32
    conc, mass, inverse = advect_x(
        extended(x_ref[lev]), extended(met[0, lev].astype(f32)), extended(met[1, lev].astype(f32))
    )
    conc1[lev] = conc
    mass1[lev] = mass
    inverse1[lev] = inverse


def latitude(lev, met, conc1, mass1, inverse1, side_c, side_i, side_f, highest):
    row = lax.broadcasted_iota(jnp.int32, (ROWS, WIDE), 0)
    first, last = row == 0, row == ROWS - 1

    def spread(ref, *at):
        return jnp.broadcast_to(ref[(*at, pl.ds(lev, 1), slice(None))].reshape(1, WIDE), (ROWS, WIDE))

    conc, mass, inverse = conc1[lev], mass1[lev], inverse1[lev]
    north = jnp.where(last & highest, 0.0, padded(met[2, lev].astype(jnp.float32)))
    c_before, c_after = spread(side_c, 1), spread(side_c, 2)
    f_before = spread(side_f)
    lower = lambda v: pltpu.roll(v, 1, 0)
    higher = lambda v: pltpu.roll(v, ROWS - 1, 0)
    down = conc - jnp.where(first, c_before, lower(conc))
    rise = jnp.where(last, c_after, higher(conc)) - conc
    slope = 0.25 * doubled_slope(down, rise)
    south = jnp.where(first, f_before, lower(north))
    ahead = conc + (1.0 - north * inverse) * slope
    behind = conc - (1.0 + south * inverse) * slope
    c_out = jnp.where(first, c_before, c_after)
    low_out = jnp.where(last, conc, spread(side_c, 0))
    high_out = jnp.where(first, conc, spread(side_c, 3))
    f_out = jnp.where(first, f_before, north)
    i_out = jnp.where(first, spread(side_i, 0), spread(side_i, 1))
    s_out = 0.25 * doubled_slope(c_out - low_out, high_out - c_out)
    from_out = c_out + (jnp.where(first, 1.0, -1.0) - f_out * i_out) * s_out
    moved = north * jnp.where(north > 0.0, ahead, jnp.where(last, from_out, higher(behind)))
    entering = f_before * jnp.where(f_before > 0.0, from_out, behind)
    new_mass = mass + south - north
    new_amount = mass * conc + jnp.where(first, entering, lower(moved)) - moved
    inverse = inverse_of(new_mass)
    return new_amount * inverse, new_mass, inverse


def vertical(lev, carry, met, conc2, mass2, inverse2, ratio, value):
    slope, flux_below, moved_below, k_below, ratio_prev, value_prev, conc, above, mass, inverse = carry
    f32 = jnp.float32
    inside = lev < LEV - 1
    flux = jnp.where(inside, padded(met[3, lev].astype(f32)), 0.0)
    k_above = jnp.where(inside, padded(met[4, lev].astype(f32)), 0.0)
    beyond = conc2[lev + 2]
    mass_above, inverse_above = mass2[lev + 1], inverse2[lev + 1]
    slope_above = 0.25 * doubled_slope(above - conc, beyond - above)
    up = flux > 0.0
    moved = flux * jnp.where(
        up, conc + (1.0 - flux * inverse) * slope, above - (1.0 + flux * inverse_above) * slope_above
    )
    amount = mass * conc + moved_below - moved
    pivot = inverse_of(mass + flux_below - flux + k_below * (1.0 - ratio_prev) + k_above)
    ratio_here = k_above * pivot
    value_here = (amount + k_below * value_prev) * pivot
    ratio[lev] = ratio_here
    value[lev] = value_here
    return slope_above, flux, moved, k_above, ratio_here, value_here, above, beyond, mass_above, inverse_above


def in_pairs(body, carry=None):
    def both(i, carry):
        carry = body(2 * i, carry)
        return body(2 * i + 1, carry)

    return lax.fori_loop(0, LEV // 2, both, carry)


def vertical_and_solve(met, out, conc2, mass2, inverse2, ratio, value):
    zero = jnp.zeros((ROWS, WIDE), jnp.float32)
    for beyond in range(2):
        conc2[LEV + beyond] = zero
    mass2[LEV] = zero
    inverse2[LEV] = zero
    first_slope = 0.25 * doubled_slope(conc2[0], conc2[1] - conc2[0])
    start = (first_slope, zero, zero, zero, zero, zero, conc2[0], conc2[1], mass2[0], inverse2[0])
    in_pairs(lambda lev, carry: vertical(lev, carry, met, conc2, mass2, inverse2, ratio, value), start)

    def back(i, above):
        lev = LEV - 1 - i
        result = value[lev] + ratio[lev] * above
        out[lev] = result[:, :LON]
        return result

    in_pairs(back, zero)


def row_plane(stage, row):
    parts = [stage[j, pl.ds(row, LEV, stride=ROWS), :] for j in range(WIDE // LANE)]
    parts[-1] = parts[-1][:, :LON % LANE]
    return jnp.concatenate(parts, axis=1).astype(jnp.bfloat16)


def fill_stage(stage, field):
    field = field.reshape(CELLS, LON)
    for j in range(WIDE // LANE):
        width = min(LANE, LON - j * LANE)
        stage[j, :, :width] = field[:, j * LANE:j * LANE + width]


def step_kernel(
    shift, x_hbm, mass_ref, flux_ref, coup_ref, out,
    x_ref, met, edge, halo, hsend, proxy, esend, stage,
    conc1, mass1, inverse1, conc2, mass2, inverse2, ratio, value, side_c, side_i, side_f,
    local_sem, main_recv, main_send, halo_recv, halo_send, proxy_sem, edge_recv, edge_send,
):
    b = lax.axis_index("band")
    t = lax.axis_index("tracer")
    z = t // 2
    c = t % 2
    root = (b + shift) % SLOTS
    k = root // 2
    line_core = root % 2
    relay = c == line_core
    speaker = c != line_core
    at_root = z == k
    is_root = relay & at_root
    passes = relay & jnp.logical_not(at_root)
    mate = t + 1 - 2 * c
    has_below = b > 0
    has_above = b < BANDS - 1

    side = jnp.where(z >= k, 1, -1)
    pos = jnp.where(z >= k, z - k, k - z)
    length = jnp.where(z >= k, CHIPS - 1 - k, k)
    hub = passes & (pos % 2 == 0)
    child_far = hub & (pos + 2 <= length)
    child_back = hub
    child_last = hub & (pos + 1 == length)
    odd_parent = jnp.where(pos < length, pos + 1, pos - 1)
    parent_pos = jnp.where(pos % 2 == 0, pos - 2, odd_parent)
    up_step = jnp.minimum(CHIPS - 1 - k, 2)
    down_step = jnp.minimum(k, 2)
    root_up = is_root & (up_step > 0)
    root_down = is_root & (down_step > 0)

    edge_hub = speaker & ((z == 2) | (z == 5))
    edge_leaf = speaker & (z != 2) & (z != 5)
    hub_z = jnp.where(z < 4, 2, 5)
    far_z = jnp.where(z == 2, 0, 7)
    tells = speaker & at_root

    def one(flag):
        return jnp.where(flag, 1, 0)

    barrier = pltpu.get_barrier_semaphore()

    def greet(band, tracer, flag=None):
        def go():
            pl.semaphore_signal(barrier, inc=1, device_id={"band": band, "tracer": tracer}, device_id_type=MESH)

        if flag is None:
            go()
        else:
            pl.when(flag)(go)

    def speaker_at_root(band):
        holder = (band + shift + SLOTS) % SLOTS
        return holder + 1 - 2 * (holder % 2)

    neighbour = jnp.where(relay, t, mate)
    greet(b, mate)
    greet(b, (k + side * parent_pos) * 2 + c, passes)
    greet(b - 1, neighbour, has_below)
    greet(b + 1, neighbour, has_above)
    greet(b, hub_z * 2 + c, edge_leaf)
    greet(b - 1, speaker_at_root(b - 1), edge_hub & has_below)
    greet(b + 1, speaker_at_root(b + 1), edge_hub & has_above)

    x_load = pltpu.make_async_copy(x_hbm, x_ref, local_sem.at[3])
    x_load.start()

    loads = (
        pltpu.make_async_copy(mass_ref.at[0], met.at[0], local_sem.at[0]),
        pltpu.make_async_copy(flux_ref.at[0], met.at[pl.ds(1, 3)], local_sem.at[1]),
        pltpu.make_async_copy(coup_ref.at[0], met.at[4], local_sem.at[2]),
    )

    @pl.when(is_root)
    def _():
        for load in loads:
            load.start()

    x_load.wait()
    fill_stage(stage, x_ref[...])
    for plane, row in enumerate((ROWS - 2, ROWS - 1, 0, 1)):
        hsend[plane] = row_plane(stage, row)

    neighbours = one(has_below) + one(has_above)
    pl.semaphore_wait(
        barrier,
        1
        + one(child_far) + one(child_back) + one(child_last)
        + one(root_up) + one(root_down)
        + 2 * one(speaker) * neighbours
        + 3 * one(edge_hub)
        + 2 * one(tells) * neighbours,
    )

    def remote(src, dst, send_sem, recv_sem, band, tracer):
        return pltpu.make_async_remote_copy(
            src_ref=src, dst_ref=dst, send_sem=send_sem, recv_sem=recv_sem,
            device_id={"band": band, "tracer": tracer}, device_id_type=MESH,
        )

    def main_copy(i, which, tracer):
        piece = met.at[i // PER_FIELD, pl.ds(i % PER_FIELD * CHUNK, CHUNK)]
        return remote(piece, piece, main_send.at[which, i], main_recv.at[i], b, tracer)

    def start_if(flag, copy):
        pl.when(flag)(copy.start)

    proxy_copy = remote(hsend, proxy, proxy_sem.at[0], proxy_sem.at[1], b, mate)

    @pl.when(is_root)
    def _():
        def send(i, _):
            start_if(root_up, main_copy(i, 0, (z + up_step) * 2 + c))
            start_if(root_down, main_copy(i, 1, (z - down_step) * 2 + c))
            main_copy(i, 3, mate).start()
            return 0

        for load, lower, upper in zip(loads, (0, 1, 4), (1, 4, 5), strict=True):
            load.wait()
            lax.fori_loop(lower * PER_FIELD, upper * PER_FIELD, send, 0)

    @pl.when(relay)
    def _():
        proxy_copy.start()

    def handed(i):
        return (
            (child_far, main_copy(i, 0, (z + 2 * side) * 2 + c)),
            (child_back, main_copy(i, 1, (z - side) * 2 + c)),
            (child_last, main_copy(i, 2, (z + side) * 2 + c)),
            (None, main_copy(i, 3, mate)),
        )

    def pass_on(i, _):
        main_copy(i, 0, mate).wait_recv()
        for flag, copy in handed(i):
            if flag is None:
                copy.start()
            else:
                start_if(flag, copy)
        return 0

    def levels(j, _):
        for lev in (2 * j, 2 * j + 1):
            longitude(lev, x_ref, met, conc1, mass1, inverse1)
        return 0

    @pl.when(passes)
    def _():
        lax.fori_loop(0, 2 * PER_FIELD, pass_on, 0)

        def both(j, _):
            pass_on(2 * PER_FIELD + j, 0)
            return levels(j, 0)

        lax.fori_loop(0, LEV // 2, both, 0)
        lax.fori_loop(2 * PER_FIELD + LEV // 2, NCHUNK, pass_on, 0)

    @pl.when(is_root)
    def _():
        lax.fori_loop(0, LEV // 2, levels, 0)

    def halo_copy(lower, own, band, tracer):
        part = pl.ds(0 if lower else 2, 2)
        return remote(
            (hsend if own else proxy).at[part], halo.at[part],
            halo_send.at[0 if own else 1, 0 if lower else 1], halo_recv.at[0 if lower else 1], band, tracer,
        )

    halos = tuple(
        (flag, halo_copy(lower, own, band, t if own else mate))
        for own in (True, False)
        for lower, band, flag in ((True, b + 1, has_above), (False, b - 1, has_below))
    )

    def edge_copy(which, lower, band, tracer, own):
        part = pl.ds(0, BELOW) if lower else pl.ds(BELOW, ABOVE)
        return remote(
            (esend if own else edge).at[part], edge.at[part],
            edge_send.at[which], edge_recv.at[0 if lower else 1], band, tracer,
        )

    edge_out = tuple(
        (tells & flag, edge_copy(which + (0 if lower else 1), lower, band, chip * 2 + line_core, True))
        for which, chip in ((0, 2), (2, 5))
        for lower, band, flag in ((True, b + 1, has_above), (False, b - 1, has_below))
    )

    def edge_relay(lower):
        first = 4 if lower else 8
        return (
            (edge_hub, edge_copy(first, lower, b, (z - 1) * 2 + c, False)),
            (edge_hub, edge_copy(first + 1, lower, b, (z + 1) * 2 + c, False)),
            (edge_hub, edge_copy(first + 2, lower, b, far_z * 2 + c, False)),
            (None, edge_copy(first + 3, lower, b, mate, False)),
        )

    sides = ((True, has_below), (False, has_above))

    @pl.when(speaker)
    def _():
        for flag, copy in halos[:2]:
            start_if(flag, copy)
        proxy_copy.wait_recv()
        for flag, copy in halos[2:]:
            start_if(flag, copy)

        @pl.when(at_root)
        def _():
            plan = (
                (0, ((ROWS - 2, 0), (ROWS - 1, 1), (0, 5), (1, 6))),
                (1, ((ROWS - 2, 2), (ROWS - 1, 3), (0, 7), (1, 8))),
                (2, ((ROWS - 1, 4),)),
            )
            for field, places in plan:
                for i in range(PER_FIELD):
                    main_copy(field * PER_FIELD + i, 0, mate).wait_recv()
                fill_stage(stage, met[field].astype(jnp.float32))
                for row, place in places:
                    esend[place] = row_plane(stage, row)
            for flag, copy in edge_out:
                start_if(flag, copy)

        for lower, present in sides:
            @pl.when(present)
            def _(lower=lower):
                edge_copy(0, lower, b, mate, False).wait_recv()
                for flag, copy in edge_relay(lower):
                    if flag is None:
                        copy.start()
                    else:
                        start_if(flag, copy)

        def arrived(i, _):
            main_copy(i, 0, mate).wait_recv()
            return 0

        first = jnp.where(at_root, 3 * PER_FIELD, 0)
        lax.fori_loop(first, jnp.maximum(first, 2 * PER_FIELD), arrived, 0)
        lax.fori_loop(0, LEV // 2, levels, 0)
        lax.fori_loop(jnp.maximum(first, 2 * PER_FIELD), NCHUNK, arrived, 0)

    @pl.when(relay)
    def _():
        for lower, present in sides:
            pl.when(present)(edge_copy(0, lower, b, mate, False).wait_recv)

    for lower, present in sides:
        pl.when(present)(halo_copy(lower, True, b, mate).wait_recv)

    lowest, highest = b == 0, b == BANDS - 1
    side_planes(edge, halo, side_c, side_i, side_f, lowest, highest)

    def across(i, _):
        for lev in (2 * i, 2 * i + 1):
            conc2[lev], mass2[lev], inverse2[lev] = latitude(
                lev, met, conc1, mass1, inverse1, side_c, side_i, side_f, highest
            )
        return 0

    lax.fori_loop(0, LEV // 2, across, 0)
    vertical_and_solve(met, out, conc2, mass2, inverse2, ratio, value)

    @pl.when(relay)
    def _():
        proxy_copy.wait_send()

    @pl.when(speaker)
    def _():
        for flag, copy in halos + edge_out:
            pl.when(flag)(copy.wait_send)
        for lower, present in sides:
            @pl.when(present)
            def _(lower=lower):
                for flag, copy in edge_relay(lower):
                    if flag is None:
                        copy.wait_send()
                    else:
                        pl.when(flag)(copy.wait_send)

    @pl.when(is_root)
    def _():
        def done(i, _):
            pl.when(root_up)(main_copy(i, 0, mate).wait_send)
            pl.when(root_down)(main_copy(i, 1, mate).wait_send)
            main_copy(i, 3, mate).wait_send()
            return 0

        lax.fori_loop(0, NCHUNK, done, 0)

    @pl.when(passes)
    def _():
        def done(i, _):
            for flag, copy in handed(i):
                if flag is None:
                    copy.wait_send()
                else:
                    pl.when(flag)(copy.wait_send)
            return 0

        lax.fori_loop(0, NCHUNK, done, 0)


def step(shift, tracer, mass, flux, coup):
    vmem = pl.BlockSpec(memory_space=pltpu.VMEM)
    hbm = pl.BlockSpec(memory_space=pl.ANY)
    bf16, f32 = jnp.bfloat16, jnp.float32
    return pl.pallas_call(
        functools.partial(step_kernel, shift),
        out_shape=jax.ShapeDtypeStruct((LEV, ROWS, LON), f32),
        in_specs=[hbm, hbm, hbm, hbm],
        out_specs=vmem,
        scratch_shapes=[
            pltpu.VMEM((LEV, ROWS, LON), f32),
            pltpu.VMEM((5, LEV, ROWS, LON), bf16),
            pltpu.VMEM((BELOW + ABOVE, LEV, LON), bf16),
            pltpu.VMEM((4, LEV, LON), bf16),
            pltpu.VMEM((4, LEV, LON), bf16),
            pltpu.VMEM((4, LEV, LON), bf16),
            pltpu.VMEM((BELOW + ABOVE, LEV, LON), bf16),
            pltpu.VMEM((WIDE // LANE, CELLS, LANE), f32),
            pltpu.VMEM((LEV, ROWS, WIDE), f32),
            pltpu.VMEM((LEV, ROWS, WIDE), f32),
            pltpu.VMEM((LEV, ROWS, WIDE), f32),
            pltpu.VMEM((LEV + 2, ROWS, WIDE), f32),
            pltpu.VMEM((LEV + 1, ROWS, WIDE), f32),
            pltpu.VMEM((LEV + 1, ROWS, WIDE), f32),
            pltpu.VMEM((LEV, ROWS, WIDE), f32),
            pltpu.VMEM((LEV, ROWS, WIDE), f32),
            pltpu.VMEM((4, LEV, WIDE), f32),
            pltpu.VMEM((2, LEV, WIDE), f32),
            pltpu.VMEM((LEV, WIDE), f32),
            pltpu.SemaphoreType.DMA((4,)),
            pltpu.SemaphoreType.DMA((NCHUNK,)),
            pltpu.SemaphoreType.DMA((4, NCHUNK)),
            pltpu.SemaphoreType.DMA((2,)),
            pltpu.SemaphoreType.DMA((2, 2)),
            pltpu.SemaphoreType.DMA((2,)),
            pltpu.SemaphoreType.DMA((2,)),
            pltpu.SemaphoreType.DMA((12,)),
        ],
        compiler_params=pltpu.CompilerParams(
            collective_id=shift, has_side_effects=True, vmem_limit_bytes=24 << 20
        ),
        name="transport",
    )(tracer, mass, flux, coup)


def per_device(tracer, air_mass, fluxes, diffusivity, input_slot):
    held = tracer.reshape(LEV, ROWS, LON)
    branches = [functools.partial(step, shift) for shift in range(SLOTS)]
    return lax.switch(input_slot[0], branches, held, air_mass, fluxes, diffusivity).reshape(tracer.shape)


def solution(mesh):
    placed = (
        P(None, "tracer", "band", None),
        P("tracer", None, "band", None),
        P("tracer", None, None, "band", None),
        P("tracer", None, "band", None),
        P(),
    )
    return jax.shard_map(
        per_device,
        mesh=mesh,
        in_specs=placed,
        out_specs=P(None, "tracer", "band", None),
        check_vma=False,
    )
```

```python
import functools

import jax
import jax.numpy as jnp
from jax import lax
from jax.experimental import pallas as pl
from jax.experimental.pallas import tpu as pltpu
from jax.sharding import PartitionSpec as P

MESH = pl.DeviceIdType.MESH
LEV = 16
ROWS = 8
LON = 720
WIDE = 768
LANE = 128
BANDS = 32
SLOTS = 16
CHIPS = 8
CELLS = LEV * ROWS
CHUNK = 4
PER_FIELD = LEV // CHUNK
NCHUNK = 5 * PER_FIELD
EARLY = 3 * PER_FIELD
BELOW = 5
ABOVE = 4


def extended(x):
    spare = (WIDE - LON) // 2
    return jnp.concatenate([x, x[:, :spare], x[:, LON - spare:]], axis=1)


def padded(x):
    return jnp.concatenate([x, jnp.zeros((x.shape[0], WIDE - LON), x.dtype)], axis=1)


def inverse_of(x):
    return pl.reciprocal(x, approx=True)


def doubled_slope(down, rise):
    middle = down + rise
    down, rise = 4.0 * down, 4.0 * rise
    positive = jnp.maximum(jnp.minimum(jnp.minimum(middle, down), rise), 0.0)
    negative = jnp.minimum(jnp.maximum(jnp.maximum(middle, down), rise), 0.0)
    return positive + negative


def advect_x(conc, mass, east):
    left = lambda v: pltpu.roll(v, 1, 1)
    right = lambda v: pltpu.roll(v, WIDE - 1, 1)
    rise = right(conc) - conc
    slope = 0.25 * doubled_slope(left(rise), rise)
    inverse = inverse_of(mass)
    west = left(east)
    ahead = conc + (1.0 - east * inverse) * slope
    behind = conc - (1.0 + west * inverse) * slope
    moved = east * jnp.where(east > 0.0, ahead, right(behind))
    new_mass = mass + west - east
    new_amount = mass * conc + left(moved) - moved
    inverse = inverse_of(new_mass)
    return new_amount * inverse, new_mass, inverse


def side_planes(edge, halo, side_c, side_i, side_f, lowest, highest):
    f32 = jnp.float32

    def plane(i):
        return extended(edge[i].astype(f32))

    def one_row(at, _):
        upper = at // 2
        mass_at = at + 3 * upper
        conc, _, inverse = advect_x(extended(halo[at].astype(f32)), plane(mass_at), plane(mass_at + 2))
        out_of = jnp.where(upper == 1, highest, lowest)
        side_c[at] = jnp.where(out_of, 0.0, conc)
        side_i[at] = jnp.where(out_of, 1.0, inverse)
        return 0

    lax.fori_loop(0, 4, one_row, 0)
    side_f[...] = jnp.where(lowest, 0.0, plane(4))


def longitude(lev, x_ref, met, conc1, mass1, inverse1):
    f32 = jnp.float32
    conc, mass, inverse = advect_x(
        extended(x_ref[lev]), extended(met[0, lev].astype(f32)), extended(met[1, lev].astype(f32))
    )
    conc1[lev] = conc
    mass1[lev] = mass
    inverse1[lev] = inverse


def latitude(lev, met, conc1, mass1, inverse1, side_c, side_i, side_f, highest):
    row = lax.broadcasted_iota(jnp.int32, (ROWS, WIDE), 0)
    first, last = row == 0, row == ROWS - 1

    def spread(ref, *at):
        return jnp.broadcast_to(ref[(*at, pl.ds(lev, 1), slice(None))].reshape(1, WIDE), (ROWS, WIDE))

    conc, mass, inverse = conc1[lev], mass1[lev], inverse1[lev]
    north = jnp.where(last & highest, 0.0, padded(met[2, lev].astype(jnp.float32)))
    c_before, c_after = spread(side_c, 1), spread(side_c, 2)
    f_before = spread(side_f)
    lower = lambda v: pltpu.roll(v, 1, 0)
    higher = lambda v: pltpu.roll(v, ROWS - 1, 0)
    down = conc - jnp.where(first, c_before, lower(conc))
    rise = jnp.where(last, c_after, higher(conc)) - conc
    slope = 0.25 * doubled_slope(down, rise)
    south = jnp.where(first, f_before, lower(north))
    ahead = conc + (1.0 - north * inverse) * slope
    behind = conc - (1.0 + south * inverse) * slope
    c_out = jnp.where(first, c_before, c_after)
    low_out = jnp.where(last, conc, spread(side_c, 0))
    high_out = jnp.where(first, conc, spread(side_c, 3))
    f_out = jnp.where(first, f_before, north)
    i_out = jnp.where(first, spread(side_i, 1), spread(side_i, 2))
    s_out = 0.25 * doubled_slope(c_out - low_out, high_out - c_out)
    from_out = c_out + (jnp.where(first, 1.0, -1.0) - f_out * i_out) * s_out
    moved = north * jnp.where(north > 0.0, ahead, jnp.where(last, from_out, higher(behind)))
    entering = f_before * jnp.where(f_before > 0.0, from_out, behind)
    new_mass = mass + south - north
    new_amount = mass * conc + jnp.where(first, entering, lower(moved)) - moved
    inverse = inverse_of(new_mass)
    return new_amount * inverse, new_mass, inverse


def vertical(lev, carry, met, conc2, mass2, inverse2, ratio, value):
    slope, flux_below, moved_below, k_below, ratio_prev, value_prev, conc, above, mass, inverse = carry
    f32 = jnp.float32
    inside = lev < LEV - 1
    flux = jnp.where(inside, padded(met[3, lev].astype(f32)), 0.0)
    k_above = jnp.where(inside, padded(met[4, lev].astype(f32)), 0.0)
    beyond = conc2[lev + 2]
    mass_above, inverse_above = mass2[lev + 1], inverse2[lev + 1]
    slope_above = 0.25 * doubled_slope(above - conc, beyond - above)
    up = flux > 0.0
    moved = flux * jnp.where(
        up, conc + (1.0 - flux * inverse) * slope, above - (1.0 + flux * inverse_above) * slope_above
    )
    amount = mass * conc + moved_below - moved
    pivot = inverse_of(mass + flux_below - flux + k_below * (1.0 - ratio_prev) + k_above)
    ratio_here = k_above * pivot
    value_here = (amount + k_below * value_prev) * pivot
    ratio[lev] = ratio_here
    value[lev] = value_here
    return slope_above, flux, moved, k_above, ratio_here, value_here, above, beyond, mass_above, inverse_above


def row_plane(stage, row):
    parts = [stage[j, pl.ds(row, LEV, stride=ROWS), :] for j in range(WIDE // LANE)]
    parts[-1] = parts[-1][:, :LON % LANE]
    return jnp.concatenate(parts, axis=1).astype(jnp.bfloat16)


def fill_stage(stage, field):
    field = field.reshape(CELLS, LON)
    for j in range(WIDE // LANE):
        width = min(LANE, LON - j * LANE)
        stage[j, :, :width] = field[:, j * LANE:j * LANE + width]


def stride_tree(z, entry):
    pos, length = z - entry, CHIPS - 1 - entry
    even = pos % 2 == 0
    parent_pos = jnp.where(even, pos - 2, jnp.where(pos < length, pos + 1, pos - 1))
    return entry + parent_pos, even & (pos < length), even, z + jnp.minimum(2, length - pos)


def step_kernel(
    shift, x_hbm, mass_ref, flux_ref, coup_ref, out,
    x_ref, met, edge, halo, hsend, proxy, esend, stage,
    conc1, mass1, inverse1, conc2, mass2, inverse2, ratio, value, side_c, side_i, side_f,
    local_sem, out_sem, main_recv, main_send, halo_recv, halo_send, proxy_sem, edge_recv, edge_send,
):
    b = lax.axis_index("band")
    t = lax.axis_index("tracer")
    z = t // 2
    c = t % 2
    root = (b + shift) % SLOTS
    k = root // 2
    line_core = root % 2
    relay = c == line_core
    speaker = c != line_core
    at_root = z == k
    is_root = relay & at_root
    passes = relay & jnp.logical_not(at_root)
    mate = t + 1 - 2 * c
    has_below = b > 0
    has_above = b < BANDS - 1

    above = z > k
    pos = jnp.where(above, z - k, k - z)
    length = jnp.where(above, CHIPS - 1 - k, k)
    middle = (length + 1) // 2
    after = length - middle
    at_middle = passes & jnp.logical_not(above) & (pos == middle)
    at_far = passes & jnp.logical_not(above) & (pos == middle + 2)
    beyond_parent = jnp.where((after == 1) | (pos == middle + 2), middle, middle + 2)
    down_parent = k - jnp.where(pos == middle, 0, jnp.where(pos < middle, pos + 1, beyond_parent))
    stride_parent, stride_on, stride_back, stride_to = stride_tree(z, k)
    main_parent = jnp.where(above, stride_parent, down_parent)
    down_on = (at_middle & (after >= 1)) | (at_far & (length >= middle + 3))
    down_back = (at_middle & (middle >= 2)) | (passes & jnp.logical_not(above) & (pos < middle) & (pos >= 2)) | at_far
    child_on = jnp.where(above, passes & stride_on, down_on)
    child_back = jnp.where(above, passes & stride_back, down_back)
    on_to = jnp.where(above, stride_to, z - jnp.where(at_middle & (after >= 2), 2, 1))
    back_to = jnp.where(above, z - 1, z + 1)
    leaf = passes & jnp.logical_not(child_on | child_back)
    root_up = is_root & (k < CHIPS - 1)
    root_down = is_root & (k > 0)
    up_to = jnp.minimum(k + 2, CHIPS - 1)
    down_to = k - (k + 1) // 2

    entry = z // 4 * 4 + 1
    at_entry = speaker & (z == entry)
    edge_on = speaker & ((z == entry) | (z == entry + 1))
    edge_back = at_entry
    edge_parent = jnp.where(z == entry + 2, z - 1, entry)

    tells = speaker & at_root

    def one(flag):
        return jnp.where(flag, 1, 0)

    barrier = pltpu.get_barrier_semaphore()

    def greet(band, tracer, flag=None):
        def go():
            pl.semaphore_signal(barrier, inc=1, device_id={"band": band, "tracer": tracer}, device_id_type=MESH)

        if flag is None:
            go()
        else:
            pl.when(flag)(go)

    def speaker_at_root(band):
        holder = (band + shift + SLOTS) % SLOTS
        return holder + 1 - 2 * (holder % 2)

    neighbour = jnp.where(relay, t, mate)
    greet(b, mate)
    greet(b, main_parent * 2 + c, passes)
    greet(b - 1, neighbour, has_below)
    greet(b + 1, neighbour, has_above)
    greet(b, edge_parent * 2 + c, speaker & jnp.logical_not(at_entry))
    greet(b - 1, speaker_at_root(b - 1), at_entry & has_below)
    greet(b + 1, speaker_at_root(b + 1), at_entry & has_above)

    x_load = pltpu.make_async_copy(x_hbm, x_ref, local_sem.at[3])
    x_load.start()

    loads = (
        pltpu.make_async_copy(mass_ref.at[0], met.at[0], local_sem.at[0]),
        pltpu.make_async_copy(flux_ref.at[0], met.at[pl.ds(1, 3)], local_sem.at[1]),
        pltpu.make_async_copy(coup_ref.at[0], met.at[4], local_sem.at[2]),
    )

    @pl.when(is_root)
    def _():
        for load in loads:
            load.start()

    neighbours = one(has_below) + one(has_above)

    def joined():
        pl.semaphore_wait(
            barrier,
            1
            + one(child_on) + one(child_back)
            + one(root_up) + one(root_down)
            + 2 * one(speaker) * neighbours
            + one(edge_on) + one(edge_back)
            + 2 * one(tells) * neighbours,
        )

    def remote(src, dst, send_sem, recv_sem, band, tracer):
        return pltpu.make_async_remote_copy(
            src_ref=src, dst_ref=dst, send_sem=send_sem, recv_sem=recv_sem,
            device_id={"band": band, "tracer": tracer}, device_id_type=MESH,
        )

    def piece_of(i):
        late = i >= EARLY
        which = jnp.where(late, 3 + (i - EARLY) % 2, i // PER_FIELD)
        group = jnp.where(late, (i - EARLY) // 2, i % PER_FIELD)
        return which, pl.ds(group * CHUNK, CHUNK)

    def main_copy(i, which, tracer, src=None):
        piece = met.at[piece_of(i)]
        return remote(piece if src is None else src, piece, main_send.at[which, i], main_recv.at[i], b, tracer)

    def start_if(flag, copy):
        pl.when(flag)(copy.start)

    mate_first = b % 2 == 1

    def send_line(i, src):
        start_if(root_up, main_copy(i, 0, up_to * 2 + c, src))
        start_if(root_down, main_copy(i, 1, down_to * 2 + c, src))

    def send_mate(i, src):
        main_copy(i, 2, mate, src).start()

    def mass_piece(i):
        return mass_ref.at[0, piece_of(i)[1]]

    def flux_piece(i):
        which, part = piece_of(i)
        return flux_ref.at[0, which - 1, part]

    def coupling_piece(i):
        return coup_ref.at[0, piece_of(i)[1]]

    def each(lower, upper, stride, body):
        def go(i, _):
            body(lower + i * stride)
            return 0

        count = upper - lower
        lax.fori_loop(0, (count if isinstance(count, int) else CHUNK) // stride, go, 0)

    @pl.when(is_root)
    def _():
        joined()

        @pl.when(mate_first)
        def _():
            each(0, PER_FIELD, 1, lambda i: send_mate(i, mass_piece(i)))
            each(PER_FIELD, EARLY, 1, lambda i: send_mate(i, flux_piece(i)))

        def send(i, src):
            send_line(i, src)

            @pl.when(jnp.logical_not(mate_first))
            def _():
                send_mate(i, src)

        each(0, PER_FIELD, 1, lambda i: send(i, mass_piece(i)))
        each(PER_FIELD, EARLY, 1, lambda i: send(i, flux_piece(i)))

        def last(i):
            for at, src in ((i, flux_piece(i)), (i + 1, coupling_piece(i + 1))):
                send_line(at, src)
                send_mate(at, src)

        each(EARLY, NCHUNK, 2, last)

    x_load.wait()
    fill_stage(stage, x_ref[...])
    for plane, row in enumerate((ROWS - 2, ROWS - 1, 0, 1)):
        hsend[plane] = row_plane(stage, row)

    pl.when(jnp.logical_not(is_root))(joined)

    proxy_copy = remote(hsend, proxy, proxy_sem.at[0], proxy_sem.at[1], b, mate)

    @pl.when(relay)
    def _():
        proxy_copy.start()

    def handed(i):
        return (
            (child_on, main_copy(i, 0, on_to * 2 + c)),
            (child_back, main_copy(i, 1, back_to * 2 + c)),
            (None, main_copy(i, 2, mate)),
        )

    def arrive(i):
        main_copy(i, 0, mate).wait_recv()

    def pass_on(i):
        arrive(i)
        for flag, copy in handed(i):
            if flag is None:
                copy.start()
            else:
                start_if(flag, copy)

    @pl.when(passes)
    def _():
        each(0, 2 * PER_FIELD, 1, pass_on)

    def halo_copy(lower, own, band, tracer):
        part = pl.ds(0 if lower else 2, 2)
        return remote(
            (hsend if own else proxy).at[part], halo.at[part],
            halo_send.at[0 if own else 1, 0 if lower else 1], halo_recv.at[0 if lower else 1], band, tracer,
        )

    halos = tuple(
        (flag, halo_copy(lower, own, band, t if own else mate))
        for own in (True, False)
        for lower, band, flag in ((True, b + 1, has_above), (False, b - 1, has_below))
    )

    parts = ((0, 2, True), (5, 2, False), (2, 3, True), (7, 2, False))

    def edge_copy(which, at, band, tracer, own):
        first, count, _ = parts[at]
        part = pl.ds(first, count)
        return remote(
            (esend if own else edge).at[part], edge.at[part], edge_send.at[which, at], edge_recv.at[at], band, tracer
        )

    def edge_out(at):
        lower = parts[at][2]
        band = b + 1 if lower else b - 1
        flag = tells & (has_above if lower else has_below)
        return tuple((flag, edge_copy(3 + half, at, band, (4 * half + 1) * 2 + line_core, True)) for half in (0, 1))

    def edge_relay(at):
        return (
            (edge_on, edge_copy(0, at, b, (z + 1) * 2 + c, False)),
            (edge_back, edge_copy(1, at, b, (z - 1) * 2 + c, False)),
            (None, edge_copy(2, at, b, mate, False)),
        )

    def tell(at):
        for flag, copy in edge_out(at):
            start_if(flag, copy)

    def has_part(at):
        return has_below if parts[at][2] else has_above

    sides = ((True, has_below), (False, has_above))

    def take_edges():
        for at in range(4):
            @pl.when(has_part(at))
            def _(at=at):
                edge_copy(0, at, b, mate, False).wait_recv()
                for flag, copy in edge_relay(at):
                    if flag is None:
                        copy.start()
                    else:
                        start_if(flag, copy)

    @pl.when(speaker)
    def _():
        for flag, copy in halos[:2]:
            start_if(flag, copy)
        proxy_copy.wait_recv()
        for flag, copy in halos[2:]:
            start_if(flag, copy)

        @pl.when(at_root)
        def _():
            plan = (
                (0, ((ROWS - 2, 0), (ROWS - 1, 1), (0, 5), (1, 6))),
                (1, ((ROWS - 2, 2), (ROWS - 1, 3), (0, 7), (1, 8))),
                (2, ((ROWS - 1, 4),)),
            )
            for field, places in plan:
                each(field * PER_FIELD, (field + 1) * PER_FIELD, 1, arrive)
                fill_stage(stage, met[field].astype(jnp.float32))
                for row, place in places:
                    esend[place] = row_plane(stage, row)
                if field == 0:
                    tell(0)
                    tell(1)
            tell(2)
            tell(3)

        pl.when(edge_on)(take_edges)
        pl.when(jnp.logical_not(at_root))(lambda: each(0, 2 * PER_FIELD, 1, arrive))

    @pl.when(is_root)
    def _():
        for load in loads:
            load.wait()

    def along(group):
        pl.when(passes)(lambda: pass_on(2 * PER_FIELD + group))
        pl.when(speaker & jnp.logical_not(at_root))(lambda: arrive(2 * PER_FIELD + group))

        def pair(lower):
            for lev in (lower, lower + 1):
                longitude(lev, x_ref, met, conc1, mass1, inverse1)

        each(group * CHUNK, (group + 1) * CHUNK, 2, pair)

    each(0, PER_FIELD, 1, along)
    pl.when(speaker & jnp.logical_not(edge_on))(take_edges)
    pl.when(passes & jnp.logical_not(leaf))(lambda: each(EARLY, NCHUNK, 1, pass_on))

    @pl.when(relay)
    def _():
        for at in range(4):
            pl.when(has_part(at))(edge_copy(0, at, b, mate, False).wait_recv)

    for lower, present in sides:
        pl.when(present)(halo_copy(lower, True, b, mate).wait_recv)

    lowest, highest = b == 0, b == BANDS - 1
    side_planes(edge, halo, side_c, side_i, side_f, lowest, highest)

    def across(i, _):
        for lev in (2 * i, 2 * i + 1):
            conc2[lev], mass2[lev], inverse2[lev] = latitude(
                lev, met, conc1, mass1, inverse1, side_c, side_i, side_f, highest
            )
        return 0

    lax.fori_loop(0, LEV // 2, across, 0)
    zero = jnp.zeros((ROWS, WIDE), jnp.float32)
    for beyond in range(2):
        conc2[LEV + beyond] = zero
    mass2[LEV] = zero
    inverse2[LEV] = zero

    def eliminate(group, carry):
        @pl.when(leaf)
        def _():
            pass_on(EARLY + 2 * group)
            pass_on(EARLY + 2 * group + 1)

        @pl.when(speaker)
        def _():
            arrive(EARLY + 2 * group)
            arrive(EARLY + 2 * group + 1)

        def pair(i, carry):
            for lev in (0, 1):
                carry = vertical(group * CHUNK + 2 * i + lev, carry, met, conc2, mass2, inverse2, ratio, value)
            return carry

        return lax.fori_loop(0, CHUNK // 2, pair, carry)

    first_slope = 0.25 * doubled_slope(conc2[0], conc2[1] - conc2[0])
    start = (first_slope, zero, zero, zero, zero, zero, conc2[0], conc2[1], mass2[0], inverse2[0])
    lax.fori_loop(0, PER_FIELD, eliminate, start)

    def result(group):
        part = pl.ds(group * CHUNK, CHUNK)
        return pltpu.make_async_copy(x_ref.at[part], out.at[part], out_sem.at[group])

    def back(i, above):
        group = PER_FIELD - 1 - i
        for lev in range(CHUNK - 1, -1, -1):
            lev = group * CHUNK + lev
            above = value[lev] + ratio[lev] * above
            x_ref[lev] = above[:, :LON]
        result(group).start()
        return above

    lax.fori_loop(0, PER_FIELD, back, zero)
    each(0, PER_FIELD, 1, lambda i: result(i).wait())

    @pl.when(relay)
    def _():
        proxy_copy.wait_send()

    @pl.when(speaker)
    def _():
        for flag, copy in halos:
            pl.when(flag)(copy.wait_send)
        for at in range(4):
            for flag, copy in edge_out(at):
                pl.when(flag)(copy.wait_send)

            @pl.when(has_part(at))
            def _(at=at):
                for flag, copy in edge_relay(at):
                    if flag is None:
                        copy.wait_send()
                    else:
                        pl.when(flag)(copy.wait_send)

    @pl.when(is_root)
    def _():
        def done(i):
            pl.when(root_up)(main_copy(i, 0, mate).wait_send)
            pl.when(root_down)(main_copy(i, 1, mate).wait_send)
            main_copy(i, 2, mate).wait_send()

        each(0, NCHUNK, 1, done)

    @pl.when(passes)
    def _():
        def done(i):
            for flag, copy in handed(i):
                if flag is None:
                    copy.wait_send()
                else:
                    pl.when(flag)(copy.wait_send)

        each(0, NCHUNK, 1, done)


def step(shift, tracer, mass, flux, coup):
    hbm = pl.BlockSpec(memory_space=pl.ANY)
    bf16, f32 = jnp.bfloat16, jnp.float32
    return pl.pallas_call(
        functools.partial(step_kernel, shift),
        out_shape=jax.ShapeDtypeStruct((LEV, ROWS, LON), f32),
        in_specs=[hbm, hbm, hbm, hbm],
        out_specs=hbm,
        scratch_shapes=[
            pltpu.VMEM((LEV, ROWS, LON), f32),
            pltpu.VMEM((5, LEV, ROWS, LON), bf16),
            pltpu.VMEM((BELOW + ABOVE, LEV, LON), bf16),
            pltpu.VMEM((4, LEV, LON), bf16),
            pltpu.VMEM((4, LEV, LON), bf16),
            pltpu.VMEM((4, LEV, LON), bf16),
            pltpu.VMEM((BELOW + ABOVE, LEV, LON), bf16),
            pltpu.VMEM((WIDE // LANE, CELLS, LANE), f32),
            pltpu.VMEM((LEV, ROWS, WIDE), f32),
            pltpu.VMEM((LEV, ROWS, WIDE), f32),
            pltpu.VMEM((LEV, ROWS, WIDE), f32),
            pltpu.VMEM((LEV + 2, ROWS, WIDE), f32),
            pltpu.VMEM((LEV + 1, ROWS, WIDE), f32),
            pltpu.VMEM((LEV + 1, ROWS, WIDE), f32),
            pltpu.VMEM((LEV, ROWS, WIDE), f32),
            pltpu.VMEM((LEV, ROWS, WIDE), f32),
            pltpu.VMEM((4, LEV, WIDE), f32),
            pltpu.VMEM((4, LEV, WIDE), f32),
            pltpu.VMEM((LEV, WIDE), f32),
            pltpu.SemaphoreType.DMA((4,)),
            pltpu.SemaphoreType.DMA((PER_FIELD,)),
            pltpu.SemaphoreType.DMA((NCHUNK,)),
            pltpu.SemaphoreType.DMA((3, NCHUNK)),
            pltpu.SemaphoreType.DMA((2,)),
            pltpu.SemaphoreType.DMA((2, 2)),
            pltpu.SemaphoreType.DMA((2,)),
            pltpu.SemaphoreType.DMA((4,)),
            pltpu.SemaphoreType.DMA((5, 4)),
        ],
        compiler_params=pltpu.CompilerParams(
            collective_id=shift, has_side_effects=True, vmem_limit_bytes=24 << 20
        ),
        name="transport",
    )(tracer, mass, flux, coup)


def per_device(tracer, air_mass, fluxes, diffusivity, input_slot):
    held = tracer.reshape(LEV, ROWS, LON)
    branches = [functools.partial(step, shift) for shift in range(SLOTS)]
    return lax.switch(input_slot[0], branches, held, air_mass, fluxes, diffusivity).reshape(tracer.shape)


def solution(mesh):
    placed = (
        P(None, "tracer", "band", None),
        P("tracer", None, "band", None),
        P("tracer", None, None, "band", None),
        P("tracer", None, "band", None),
        P(),
    )
    return jax.shard_map(
        per_device,
        mesh=mesh,
        in_specs=placed,
        out_specs=P(None, "tracer", "band", None),
        check_vma=False,
    )
```

```python
import functools

import jax
import jax.numpy as jnp
from jax import lax
from jax.experimental import pallas as pl
from jax.experimental.pallas import tpu as pltpu
from jax.sharding import PartitionSpec as P

MESH = pl.DeviceIdType.MESH
LEV = 16
ROWS = 8
LON = 720
WIDE = 768
LANE = 128
BANDS = 32
SLOTS = 16
CHIPS = 8
CELLS = LEV * ROWS
CHUNK = 4
PER_FIELD = LEV // CHUNK
NCHUNK = 5 * PER_FIELD
EARLY = 3 * PER_FIELD
BELOW = 5
ABOVE = 4


def extended(x):
    spare = (WIDE - LON) // 2
    return jnp.concatenate([x, x[:, :spare], x[:, LON - spare:]], axis=1)


def padded(x):
    return jnp.concatenate([x, jnp.zeros((x.shape[0], WIDE - LON), x.dtype)], axis=1)


def inverse_of(x):
    return pl.reciprocal(x, approx=True)


def doubled_slope(down, rise):
    middle = down + rise
    down, rise = 4.0 * down, 4.0 * rise
    positive = jnp.maximum(jnp.minimum(jnp.minimum(middle, down), rise), 0.0)
    negative = jnp.minimum(jnp.maximum(jnp.maximum(middle, down), rise), 0.0)
    return positive + negative


def advect_x(conc, mass, east):
    left = lambda v: pltpu.roll(v, 1, 1)
    right = lambda v: pltpu.roll(v, WIDE - 1, 1)
    rise = right(conc) - conc
    slope = 0.25 * doubled_slope(left(rise), rise)
    inverse = inverse_of(mass)
    west = left(east)
    ahead = conc + (1.0 - east * inverse) * slope
    behind = conc - (1.0 + west * inverse) * slope
    moved = east * jnp.where(east > 0.0, ahead, right(behind))
    new_mass = mass + west - east
    new_amount = mass * conc + left(moved) - moved
    inverse = inverse_of(new_mass)
    return new_amount * inverse, new_mass, inverse


def side_planes(edge, halo, side_c, side_i, side_f, lowest, highest):
    f32 = jnp.float32

    def plane(i):
        return extended(edge[i].astype(f32))

    def one_row(at, _):
        upper = at // 2
        mass_at = at + 3 * upper
        conc, _, inverse = advect_x(extended(halo[at].astype(f32)), plane(mass_at), plane(mass_at + 2))
        out_of = jnp.where(upper == 1, highest, lowest)
        side_c[at] = jnp.where(out_of, 0.0, conc)
        side_i[at] = jnp.where(out_of, 1.0, inverse)
        return 0

    lax.fori_loop(0, 4, one_row, 0)
    side_f[...] = jnp.where(lowest, 0.0, plane(4))


def longitude(lev, x_ref, met, conc1, mass1, inverse1):
    f32 = jnp.float32
    conc, mass, inverse = advect_x(
        extended(x_ref[lev]), extended(met[0, lev].astype(f32)), extended(met[1, lev].astype(f32))
    )
    conc1[lev] = conc
    mass1[lev] = mass
    inverse1[lev] = inverse


def latitude(lev, met, conc1, mass1, inverse1, side_c, side_i, side_f, highest):
    row = lax.broadcasted_iota(jnp.int32, (ROWS, WIDE), 0)
    first, last = row == 0, row == ROWS - 1

    def spread(ref, *at):
        return jnp.broadcast_to(ref[(*at, pl.ds(lev, 1), slice(None))].reshape(1, WIDE), (ROWS, WIDE))

    conc, mass, inverse = conc1[lev], mass1[lev], inverse1[lev]
    north = jnp.where(last & highest, 0.0, padded(met[2, lev].astype(jnp.float32)))
    c_before, c_after = spread(side_c, 1), spread(side_c, 2)
    f_before = spread(side_f)
    lower = lambda v: pltpu.roll(v, 1, 0)
    higher = lambda v: pltpu.roll(v, ROWS - 1, 0)
    down = conc - jnp.where(first, c_before, lower(conc))
    rise = jnp.where(last, c_after, higher(conc)) - conc
    slope = 0.25 * doubled_slope(down, rise)
    south = jnp.where(first, f_before, lower(north))
    ahead = conc + (1.0 - north * inverse) * slope
    behind = conc - (1.0 + south * inverse) * slope
    c_out = jnp.where(first, c_before, c_after)
    low_out = jnp.where(last, conc, spread(side_c, 0))
    high_out = jnp.where(first, conc, spread(side_c, 3))
    f_out = jnp.where(first, f_before, north)
    i_out = jnp.where(first, spread(side_i, 1), spread(side_i, 2))
    s_out = 0.25 * doubled_slope(c_out - low_out, high_out - c_out)
    from_out = c_out + (jnp.where(first, 1.0, -1.0) - f_out * i_out) * s_out
    moved = north * jnp.where(north > 0.0, ahead, jnp.where(last, from_out, higher(behind)))
    entering = f_before * jnp.where(f_before > 0.0, from_out, behind)
    new_mass = mass + south - north
    new_amount = mass * conc + jnp.where(first, entering, lower(moved)) - moved
    inverse = inverse_of(new_mass)
    return new_amount * inverse, new_mass, inverse


def vertical(lev, carry, met, conc2, mass2, inverse2, ratio, value):
    slope, flux_below, moved_below, k_below, ratio_prev, value_prev, conc, above, mass, inverse = carry
    f32 = jnp.float32
    inside = lev < LEV - 1
    flux = jnp.where(inside, padded(met[3, lev].astype(f32)), 0.0)
    k_above = jnp.where(inside, padded(met[4, lev].astype(f32)), 0.0)
    beyond = conc2[lev + 2]
    mass_above, inverse_above = mass2[lev + 1], inverse2[lev + 1]
    slope_above = 0.25 * doubled_slope(above - conc, beyond - above)
    up = flux > 0.0
    moved = flux * jnp.where(
        up, conc + (1.0 - flux * inverse) * slope, above - (1.0 + flux * inverse_above) * slope_above
    )
    amount = mass * conc + moved_below - moved
    pivot = inverse_of(mass + flux_below - flux + k_below * (1.0 - ratio_prev) + k_above)
    ratio_here = k_above * pivot
    value_here = (amount + k_below * value_prev) * pivot
    ratio[lev] = ratio_here
    value[lev] = value_here
    return slope_above, flux, moved, k_above, ratio_here, value_here, above, beyond, mass_above, inverse_above


def row_plane(stage, row):
    parts = [stage[j, pl.ds(row, LEV, stride=ROWS), :] for j in range(WIDE // LANE)]
    parts[-1] = parts[-1][:, :LON % LANE]
    return jnp.concatenate(parts, axis=1).astype(jnp.bfloat16)


def fill_stage(stage, field):
    field = field.reshape(CELLS, LON)
    for j in range(WIDE // LANE):
        width = min(LANE, LON - j * LANE)
        stage[j, :, :width] = field[:, j * LANE:j * LANE + width]


def stride_tree(z, entry):
    pos, length = z - entry, CHIPS - 1 - entry
    even = pos % 2 == 0
    parent_pos = jnp.where(even, pos - 2, jnp.where(pos < length, pos + 1, pos - 1))
    return entry + parent_pos, even & (pos < length), even, z + jnp.minimum(2, length - pos)


def step_kernel(
    shift, x_hbm, mass_ref, flux_ref, coup_ref, out,
    x_ref, met, edge, halo, hsend, proxy, esend, stage,
    conc1, mass1, inverse1, conc2, mass2, inverse2, ratio, value, side_c, side_i, side_f,
    local_sem, out_sem, main_recv, main_send, halo_recv, halo_send, proxy_sem, edge_recv, edge_send,
):
    b = lax.axis_index("band")
    t = lax.axis_index("tracer")
    z = t // 2
    c = t % 2
    root = (b + shift) % SLOTS
    k = root // 2
    line_core = root % 2
    relay = c == line_core
    speaker = c != line_core
    at_root = z == k
    is_root = relay & at_root
    passes = relay & jnp.logical_not(at_root)
    mate = t + 1 - 2 * c
    has_below = b > 0
    has_above = b < BANDS - 1

    above = z > k
    pos = jnp.where(above, z - k, k - z)
    length = jnp.where(above, CHIPS - 1 - k, k)
    middle = (length + 1) // 2
    after = length - middle
    at_middle = passes & jnp.logical_not(above) & (pos == middle)
    at_far = passes & jnp.logical_not(above) & (pos == middle + 2)
    beyond_parent = jnp.where((after == 1) | (pos == middle + 2), middle, middle + 2)
    down_parent = k - jnp.where(pos == middle, 0, jnp.where(pos < middle, pos + 1, beyond_parent))
    stride_parent, stride_on, stride_back, stride_to = stride_tree(z, k)
    main_parent = jnp.where(above, stride_parent, down_parent)
    down_on = (at_middle & (after >= 1)) | (at_far & (length >= middle + 3))
    down_back = (at_middle & (middle >= 2)) | (passes & jnp.logical_not(above) & (pos < middle) & (pos >= 2)) | at_far
    child_on = jnp.where(above, passes & stride_on, down_on)
    child_back = jnp.where(above, passes & stride_back, down_back)
    on_to = jnp.where(above, stride_to, z - jnp.where(at_middle & (after >= 2), 2, 1))
    back_to = jnp.where(above, z - 1, z + 1)
    leaf = passes & jnp.logical_not(child_on | child_back)
    root_up = is_root & (k < CHIPS - 1)
    root_down = is_root & (k > 0)
    up_to = jnp.minimum(k + 2, CHIPS - 1)
    down_to = k - (k + 1) // 2

    entry = z // 4 * 4 + 1
    at_entry = speaker & (z == entry)
    edge_on = speaker & ((z == entry) | (z == entry + 1))
    edge_back = at_entry
    edge_parent = jnp.where(z == entry + 2, z - 1, entry)

    tells = speaker & at_root

    def one(flag):
        return jnp.where(flag, 1, 0)

    barrier = pltpu.get_barrier_semaphore()

    def greet(band, tracer, flag=None):
        def go():
            pl.semaphore_signal(barrier, inc=1, device_id={"band": band, "tracer": tracer}, device_id_type=MESH)

        if flag is None:
            go()
        else:
            pl.when(flag)(go)

    def speaker_at_root(band):
        holder = (band + shift + SLOTS) % SLOTS
        return holder + 1 - 2 * (holder % 2)

    neighbour = jnp.where(relay, t, mate)
    greet(b, mate)
    greet(b, main_parent * 2 + c, passes)
    greet(b - 1, neighbour, has_below)
    greet(b + 1, neighbour, has_above)
    greet(b, edge_parent * 2 + c, speaker & jnp.logical_not(at_entry))
    greet(b - 1, speaker_at_root(b - 1), at_entry & has_below)
    greet(b + 1, speaker_at_root(b + 1), at_entry & has_above)

    x_load = pltpu.make_async_copy(x_hbm, x_ref, local_sem.at[3])
    x_load.start()

    loads = (
        pltpu.make_async_copy(mass_ref.at[0], met.at[0], local_sem.at[0]),
        pltpu.make_async_copy(flux_ref.at[0], met.at[pl.ds(1, 3)], local_sem.at[1]),
        pltpu.make_async_copy(coup_ref.at[0], met.at[4], local_sem.at[2]),
    )

    @pl.when(is_root)
    def _():
        for load in loads:
            load.start()

    neighbours = one(has_below) + one(has_above)

    def joined():
        pl.semaphore_wait(
            barrier,
            1
            + one(child_on) + one(child_back)
            + one(root_up) + one(root_down)
            + 2 * one(speaker) * neighbours
            + one(edge_on) + one(edge_back)
            + 2 * one(tells) * neighbours,
        )

    def remote(src, dst, send_sem, recv_sem, band, tracer):
        return pltpu.make_async_remote_copy(
            src_ref=src, dst_ref=dst, send_sem=send_sem, recv_sem=recv_sem,
            device_id={"band": band, "tracer": tracer}, device_id_type=MESH,
        )

    def piece_of(i):
        late = i >= EARLY
        which = jnp.where(late, 3 + (i - EARLY) % 2, i // PER_FIELD)
        group = jnp.where(late, (i - EARLY) // 2, i % PER_FIELD)
        return which, pl.ds(group * CHUNK, CHUNK)

    def main_copy(i, which, tracer, src=None):
        piece = met.at[piece_of(i)]
        return remote(piece if src is None else src, piece, main_send.at[which, i], main_recv.at[i], b, tracer)

    def start_if(flag, copy):
        pl.when(flag)(copy.start)

    mate_first = b % 2 == 1

    def send_line(i, src):
        start_if(root_down, main_copy(i, 1, down_to * 2 + c, src))
        start_if(root_up, main_copy(i, 0, up_to * 2 + c, src))

    def send_mate(i, src):
        main_copy(i, 2, mate, src).start()

    def mass_piece(i):
        return mass_ref.at[0, piece_of(i)[1]]

    def flux_piece(i):
        which, part = piece_of(i)
        return flux_ref.at[0, which - 1, part]

    def coupling_piece(i):
        return coup_ref.at[0, piece_of(i)[1]]

    def each(lower, upper, stride, body):
        def go(i, _):
            body(lower + i * stride)
            return 0

        count = upper - lower
        lax.fori_loop(0, (count if isinstance(count, int) else CHUNK) // stride, go, 0)

    @pl.when(is_root)
    def _():
        joined()

        @pl.when(mate_first)
        def _():
            each(0, PER_FIELD, 1, lambda i: send_mate(i, mass_piece(i)))
            each(PER_FIELD, EARLY, 1, lambda i: send_mate(i, flux_piece(i)))

        def send(i, src):
            send_line(i, src)

            @pl.when(jnp.logical_not(mate_first))
            def _():
                send_mate(i, src)

        each(0, PER_FIELD, 1, lambda i: send(i, mass_piece(i)))
        each(PER_FIELD, EARLY, 1, lambda i: send(i, flux_piece(i)))

        def last(i):
            for at, src in ((i, flux_piece(i)), (i + 1, coupling_piece(i + 1))):
                send_line(at, src)
                send_mate(at, src)

        each(EARLY, NCHUNK, 2, last)

    x_load.wait()
    fill_stage(stage, x_ref[...])
    for plane, row in enumerate((ROWS - 2, ROWS - 1, 0, 1)):
        hsend[plane] = row_plane(stage, row)

    pl.when(jnp.logical_not(is_root))(joined)

    proxy_copy = remote(hsend, proxy, proxy_sem.at[0], proxy_sem.at[1], b, mate)

    @pl.when(relay)
    def _():
        proxy_copy.start()

    def handed(i):
        return (
            (child_on, main_copy(i, 0, on_to * 2 + c)),
            (child_back, main_copy(i, 1, back_to * 2 + c)),
            (None, main_copy(i, 2, mate)),
        )

    def arrive(i):
        main_copy(i, 0, mate).wait_recv()

    def pass_on(i):
        arrive(i)
        for flag, copy in handed(i):
            if flag is None:
                copy.start()
            else:
                start_if(flag, copy)

    @pl.when(passes)
    def _():
        each(0, 2 * PER_FIELD, 1, pass_on)

    def halo_copy(lower, own, band, tracer):
        part = pl.ds(0 if lower else 2, 2)
        return remote(
            (hsend if own else proxy).at[part], halo.at[part],
            halo_send.at[0 if own else 1, 0 if lower else 1], halo_recv.at[0 if lower else 1], band, tracer,
        )

    halos = tuple(
        (flag, halo_copy(lower, own, band, t if own else mate))
        for own in (True, False)
        for lower, band, flag in ((True, b + 1, has_above), (False, b - 1, has_below))
    )

    parts = ((0, 2, True), (5, 2, False), (2, 3, True), (7, 2, False))

    def edge_copy(which, at, band, tracer, own):
        first, count, _ = parts[at]
        part = pl.ds(first, count)
        return remote(
            (esend if own else edge).at[part], edge.at[part], edge_send.at[which, at], edge_recv.at[at], band, tracer
        )

    def edge_out(at):
        lower = parts[at][2]
        band = b + 1 if lower else b - 1
        flag = tells & (has_above if lower else has_below)
        return tuple((flag, edge_copy(3 + half, at, band, (4 * half + 1) * 2 + line_core, True)) for half in (0, 1))

    def edge_relay(at):
        return (
            (edge_on, edge_copy(0, at, b, (z + 1) * 2 + c, False)),
            (edge_back, edge_copy(1, at, b, (z - 1) * 2 + c, False)),
            (None, edge_copy(2, at, b, mate, False)),
        )

    def tell(at):
        for flag, copy in edge_out(at):
            start_if(flag, copy)

    def has_part(at):
        return has_below if parts[at][2] else has_above

    sides = ((True, has_below), (False, has_above))

    def take_edges():
        for at in range(4):
            @pl.when(has_part(at))
            def _(at=at):
                edge_copy(0, at, b, mate, False).wait_recv()
                for flag, copy in edge_relay(at):
                    if flag is None:
                        copy.start()
                    else:
                        start_if(flag, copy)

    @pl.when(speaker)
    def _():
        for flag, copy in halos[:2]:
            start_if(flag, copy)
        proxy_copy.wait_recv()
        for flag, copy in halos[2:]:
            start_if(flag, copy)

        @pl.when(at_root)
        def _():
            plan = (
                (0, ((ROWS - 2, 0), (ROWS - 1, 1), (0, 5), (1, 6))),
                (1, ((ROWS - 2, 2), (ROWS - 1, 3), (0, 7), (1, 8))),
                (2, ((ROWS - 1, 4),)),
            )
            for field, places in plan:
                each(field * PER_FIELD, (field + 1) * PER_FIELD, 1, arrive)
                fill_stage(stage, met[field].astype(jnp.float32))
                for row, place in places:
                    esend[place] = row_plane(stage, row)
                if field == 0:
                    tell(0)
                    tell(1)
            tell(2)
            tell(3)

        pl.when(edge_on)(take_edges)
        pl.when(jnp.logical_not(at_root))(lambda: each(0, 2 * PER_FIELD, 1, arrive))

    @pl.when(is_root)
    def _():
        for load in loads:
            load.wait()

    def along(group):
        pl.when(passes)(lambda: pass_on(2 * PER_FIELD + group))
        pl.when(speaker & jnp.logical_not(at_root))(lambda: arrive(2 * PER_FIELD + group))

        def pair(lower):
            for lev in (lower, lower + 1):
                longitude(lev, x_ref, met, conc1, mass1, inverse1)

        each(group * CHUNK, (group + 1) * CHUNK, 2, pair)

    each(0, PER_FIELD, 1, along)
    pl.when(speaker & jnp.logical_not(edge_on))(take_edges)
    pl.when(passes & jnp.logical_not(leaf))(lambda: each(EARLY, NCHUNK, 1, pass_on))

    @pl.when(relay)
    def _():
        for at in range(4):
            pl.when(has_part(at))(edge_copy(0, at, b, mate, False).wait_recv)

    for lower, present in sides:
        pl.when(present)(halo_copy(lower, True, b, mate).wait_recv)

    lowest, highest = b == 0, b == BANDS - 1
    side_planes(edge, halo, side_c, side_i, side_f, lowest, highest)

    def across(i, _):
        for lev in (2 * i, 2 * i + 1):
            conc2[lev], mass2[lev], inverse2[lev] = latitude(
                lev, met, conc1, mass1, inverse1, side_c, side_i, side_f, highest
            )
        return 0

    lax.fori_loop(0, LEV // 2, across, 0)
    zero = jnp.zeros((ROWS, WIDE), jnp.float32)
    for beyond in range(2):
        conc2[LEV + beyond] = zero
    mass2[LEV] = zero
    inverse2[LEV] = zero

    def eliminate(group, carry):
        @pl.when(leaf)
        def _():
            pass_on(EARLY + 2 * group)
            pass_on(EARLY + 2 * group + 1)

        @pl.when(speaker)
        def _():
            arrive(EARLY + 2 * group)
            arrive(EARLY + 2 * group + 1)

        def pair(i, carry):
            for lev in (0, 1):
                carry = vertical(group * CHUNK + 2 * i + lev, carry, met, conc2, mass2, inverse2, ratio, value)
            return carry

        return lax.fori_loop(0, CHUNK // 2, pair, carry)

    first_slope = 0.25 * doubled_slope(conc2[0], conc2[1] - conc2[0])
    start = (first_slope, zero, zero, zero, zero, zero, conc2[0], conc2[1], mass2[0], inverse2[0])
    lax.fori_loop(0, PER_FIELD, eliminate, start)

    def result(group):
        part = pl.ds(group * CHUNK, CHUNK)
        return pltpu.make_async_copy(x_ref.at[part], out.at[part], out_sem.at[group])

    def back(i, above):
        group = PER_FIELD - 1 - i
        for lev in range(CHUNK - 1, -1, -1):
            lev = group * CHUNK + lev
            above = value[lev] + ratio[lev] * above
            x_ref[lev] = above[:, :LON]
        result(group).start()
        return above

    lax.fori_loop(0, PER_FIELD, back, zero)
    each(0, PER_FIELD, 1, lambda i: result(i).wait())

    @pl.when(relay)
    def _():
        proxy_copy.wait_send()

    @pl.when(speaker)
    def _():
        for flag, copy in halos:
            pl.when(flag)(copy.wait_send)
        for at in range(4):
            for flag, copy in edge_out(at):
                pl.when(flag)(copy.wait_send)

            @pl.when(has_part(at))
            def _(at=at):
                for flag, copy in edge_relay(at):
                    if flag is None:
                        copy.wait_send()
                    else:
                        pl.when(flag)(copy.wait_send)

    @pl.when(is_root)
    def _():
        def done(i):
            pl.when(root_up)(main_copy(i, 0, mate).wait_send)
            pl.when(root_down)(main_copy(i, 1, mate).wait_send)
            main_copy(i, 2, mate).wait_send()

        each(0, NCHUNK, 1, done)

    @pl.when(passes)
    def _():
        def done(i):
            for flag, copy in handed(i):
                if flag is None:
                    copy.wait_send()
                else:
                    pl.when(flag)(copy.wait_send)

        each(0, NCHUNK, 1, done)


def step(shift, tracer, mass, flux, coup):
    hbm = pl.BlockSpec(memory_space=pl.ANY)
    bf16, f32 = jnp.bfloat16, jnp.float32
    return pl.pallas_call(
        functools.partial(step_kernel, shift),
        out_shape=jax.ShapeDtypeStruct((LEV, ROWS, LON), f32),
        in_specs=[hbm, hbm, hbm, hbm],
        out_specs=hbm,
        scratch_shapes=[
            pltpu.VMEM((LEV, ROWS, LON), f32),
            pltpu.VMEM((5, LEV, ROWS, LON), bf16),
            pltpu.VMEM((BELOW + ABOVE, LEV, LON), bf16),
            pltpu.VMEM((4, LEV, LON), bf16),
            pltpu.VMEM((4, LEV, LON), bf16),
            pltpu.VMEM((4, LEV, LON), bf16),
            pltpu.VMEM((BELOW + ABOVE, LEV, LON), bf16),
            pltpu.VMEM((WIDE // LANE, CELLS, LANE), f32),
            pltpu.VMEM((LEV, ROWS, WIDE), f32),
            pltpu.VMEM((LEV, ROWS, WIDE), f32),
            pltpu.VMEM((LEV, ROWS, WIDE), f32),
            pltpu.VMEM((LEV + 2, ROWS, WIDE), f32),
            pltpu.VMEM((LEV + 1, ROWS, WIDE), f32),
            pltpu.VMEM((LEV + 1, ROWS, WIDE), f32),
            pltpu.VMEM((LEV, ROWS, WIDE), f32),
            pltpu.VMEM((LEV, ROWS, WIDE), f32),
            pltpu.VMEM((4, LEV, WIDE), f32),
            pltpu.VMEM((4, LEV, WIDE), f32),
            pltpu.VMEM((LEV, WIDE), f32),
            pltpu.SemaphoreType.DMA((4,)),
            pltpu.SemaphoreType.DMA((PER_FIELD,)),
            pltpu.SemaphoreType.DMA((NCHUNK,)),
            pltpu.SemaphoreType.DMA((3, NCHUNK)),
            pltpu.SemaphoreType.DMA((2,)),
            pltpu.SemaphoreType.DMA((2, 2)),
            pltpu.SemaphoreType.DMA((2,)),
            pltpu.SemaphoreType.DMA((4,)),
            pltpu.SemaphoreType.DMA((5, 4)),
        ],
        compiler_params=pltpu.CompilerParams(
            collective_id=shift, has_side_effects=True, vmem_limit_bytes=24 << 20
        ),
        name="transport",
    )(tracer, mass, flux, coup)


def per_device(tracer, air_mass, fluxes, diffusivity, input_slot):
    held = tracer.reshape(LEV, ROWS, LON)
    branches = [functools.partial(step, shift) for shift in range(SLOTS)]
    return lax.switch(input_slot[0], branches, held, air_mass, fluxes, diffusivity).reshape(tracer.shape)


def solution(mesh):
    placed = (
        P(None, "tracer", "band", None),
        P("tracer", None, "band", None),
        P("tracer", None, None, "band", None),
        P("tracer", None, "band", None),
        P(),
    )
    return jax.shard_map(
        per_device,
        mesh=mesh,
        in_specs=placed,
        out_specs=P(None, "tracer", "band", None),
        check_vma=False,
    )
```
